32 devices in a mesh: member: 4 (over y, core), space: 8 (over z, x).
Axes of the slice: x: 2, y: 2, z: 4, core: 2. Of those that a mesh axis runs over, the one named last changes fastest.
Arguments:
- ensemble: float32 [256, 32, 2048], P('member', None, 'space'), may hold values from -6 to 6
- obs_weight: float32 [32, 8192], P(None, 'space'), may hold values from -1 to 1
- obs_value: float32 [8192], P('space'), may hold values from -6 to 6
- obs_rinv: float32 [8192], P('space'), may hold values from 0.5 to 4
- obs_column: int32 [8192], P('space'), may hold values from 0 to 255
- set_rows: int32 [32, 512], P('space'), may hold values from 0 to 1023
- set_count: int32 [32], P('space'), may hold values from 128 to 512, as said below
- neighbour: int32 [4, 2048], P(None, 'space'), may hold values from 0 to 3
- interp_weight: float32 [4, 2048], P(None, 'space'), may hold values from 0.1 to 1
Outputs:
- analysed: float32 [256, 32, 2048], P('member', None, 'space')
The draws below stay inside these ranges and needn't reach their ends.
Inputs may be any that keep to these rules, and one draw needn't show every extreme that they name: `set_rows`: a row among the 1024 observations of the space index that owns the coarse point; coarse point j is owned by space index j // (member count). `set_count`: rows of a local set at or past its count are padding; some coarse point has the full 512 rows in every draw. `obs_column`: a column among the 256 columns of the space index that holds the observation. `neighbour`: a coarse point among those owned by the column's own space index, numbered from 0.
All inputs are finite; a program needn't handle non-finite values.
Results may differ from the reference program's by a relative error of at most 0.0035.
Values may be sent and summed in bfloat16 or wider, within the bound.
A program may use at most 64 MiB of HBM per device.

```python
import math
import jax
import jax.numpy as jnp
from jax import lax

K = 256
NV = 32
LSET = 512
NB = 4
NS_ITERS = 5
COL_DEV = 256
OBS_DEV = 1024
NCOL = 2048
NOBS = 8192
NCP = 32
N_MEMBER = 4
N_SPACE = 8


def draw_set_count(key, part):
    key_count = jax.random.fold_in(key, 11)
    key_where = jax.random.fold_in(key, 12)
    counts = jax.random.randint(key_count, (NCP,), LSET // 4, LSET + 1)
    where_full = jax.random.randint(key_where, (), 0, NCP)
    return counts.at[where_full].set(LSET).astype(jnp.int32)


def place_ends(result, own_key, smallest, high):
    spot = [jax.random.randint(jax.random.fold_in(own_key, axis), (), 0, length) for axis, length in enumerate(result.shape)]
    longest = result.shape.index(max(result.shape))
    next_to = spot[:longest] + [(spot[longest] + 1) % result.shape[longest]] + spot[longest + 1:]
    return result.at[tuple(spot)].set(smallest).at[tuple(next_to)].set(high)


def block_levels(key, dims, split, smallest, largest):
    loudness, own = 1.0, jax.random.fold_in(key, 6)
    for dim, shards_of in split:
        draws = jnp.exp(jax.random.uniform(jax.random.fold_in(own, dim), (shards_of,), jnp.float32, smallest / len(split), largest / len(split)))
        loudness = loudness * jnp.repeat(draws, dims[dim] // shards_of).reshape([-1 if axis == dim else 1 for axis in range(len(dims))])
    return loudness


def bell_draw(stream_key, extent, scale, limit, shards=(), kind=jnp.bfloat16):
    values = jax.random.normal(stream_key, extent, jnp.float32) * scale
    if len(shards) > 0:
        values = block_levels(stream_key, extent, shards, -0.22, 0.18) * values
    return jnp.clip(values, min=-limit, max=limit).astype(kind)


def setup_inputs(seed: int = 0) -> dict:
    arg_keys = jax.random.split(jax.random.key(seed), 10)
    return {
        "ensemble": bell_draw(arg_keys[0], (K, NV, NCOL), 1.0, 6.0, ((0, 4), (2, 8)), jnp.float32),
        "obs_weight": bell_draw(arg_keys[1], (NV, NOBS), NV ** -0.5, 1.0, ((1, 8),), jnp.float32),
        "obs_value": bell_draw(arg_keys[2], (NOBS,), 1.0, 6.0, ((0, 8),), jnp.float32),
        "obs_rinv": jnp.clip(jnp.exp(math.log(4.0) - 2.0794415 * jax.random.uniform(arg_keys[3], (NOBS,), jnp.float32) ** block_levels(arg_keys[3], (NOBS,), ((0, 8),), -0.2, 0.2)), 0.5, 4.0),
        "obs_column": place_ends(jax.random.randint(arg_keys[4], (NOBS,), 0, COL_DEV), jax.random.fold_in(arg_keys[4], 1), 0, COL_DEV - 1).astype(jnp.int32),
        "set_rows": place_ends(jax.random.randint(arg_keys[5], (NCP, LSET), 0, OBS_DEV), jax.random.fold_in(arg_keys[5], 1), 0, OBS_DEV - 1).astype(jnp.int32),
        "set_count": draw_set_count(jax.random.fold_in(arg_keys[9], 71), 0),
        "neighbour": place_ends(jax.random.randint(arg_keys[7], (NB, NCOL), 0, N_MEMBER), jax.random.fold_in(arg_keys[7], 1), 0, N_MEMBER - 1).astype(jnp.int32),
        "interp_weight": jnp.clip(0.1 + 0.9 * jax.random.uniform(arg_keys[8], (NB, NCOL), jnp.float32) ** block_levels(arg_keys[8], (NB, NCOL), ((1, 8),), -0.2, 0.2), 0.1, 1.0),
    }


highest = lax.Precision.HIGHEST

def make_transform(selected, obs_pick, rinv_pick, count):
    ens_size = selected.shape[0]
    set_len = selected.shape[1]
    obs_mean = lax.optimization_barrier(jnp.mean(selected, axis=0))
    anomaly = selected - obs_mean[None, :]
    innovation = obs_pick - obs_mean
    in_set = jnp.arange(set_len, dtype=jnp.int32) < count
    set_weight = jnp.where(in_set, rinv_pick, jnp.zeros_like(rinv_pick))
    identity = jnp.eye(ens_size, dtype=selected.dtype)
    posterior = (ens_size - 1.0) * identity + jnp.dot(anomaly * set_weight[None, :], anomaly.T, precision=highest)
    frob_norm = jnp.sqrt(jnp.sum(posterior * posterior))
    iterate = posterior / frob_norm
    inverse = identity
    for turn_index in range(NS_ITERS):
        ns_step = 1.5 * identity - 0.5 * jnp.dot(inverse, iterate, precision=highest)
        iterate = jnp.dot(iterate, ns_step, precision=highest)
        inverse = jnp.dot(ns_step, inverse, precision=highest)
    drive_vec = jnp.dot(anomaly, set_weight * innovation, precision=highest)
    mean_weight = jnp.dot(inverse, jnp.dot(inverse, drive_vec, precision=highest), precision=highest) / frob_norm
    spread = inverse * jnp.sqrt((ens_size - 1.0) / frob_norm)
    return (spread + mean_weight[:, None]).astype(jnp.bfloat16)

def reference(ensemble, obs_weight, obs_value, obs_rinv, obs_column, set_rows, set_count, neighbour, interp_weight):
    blocks = N_SPACE
    ens_blocks = ensemble.reshape(K, NV, blocks, COL_DEV).transpose(2, 0, 1, 3)
    weight_blocks = obs_weight.reshape(NV, blocks, OBS_DEV).transpose(1, 0, 2)
    column_blocks = obs_column.reshape(blocks, OBS_DEV)

    def project(operands):
        ens_block, weight_block, column_block = operands
        picked_vals = jnp.take(ens_block, column_block, axis=2)
        return lax.optimization_barrier(jnp.sum(picked_vals * weight_block[None], axis=1))
    observed = lax.map(project, (ens_blocks, weight_blocks, column_blocks))
    value_blocks = obs_value.reshape(blocks, OBS_DEV)
    rinv_blocks = obs_rinv.reshape(blocks, OBS_DEV)

    def analyse(coarse_id):
        block_id = coarse_id // N_MEMBER
        row_ids = set_rows[coarse_id]
        selected = jnp.take(observed[block_id], row_ids, axis=1)
        obs_pick = jnp.take(value_blocks[block_id], row_ids)
        rinv_pick = jnp.take(rinv_blocks[block_id], row_ids)
        return make_transform(selected, obs_pick, rinv_pick, set_count[coarse_id])
    transforms = lax.map(analyse, jnp.arange(NCP, dtype=jnp.int32))
    trans_blocks = transforms.reshape(blocks, N_MEMBER, K, K)
    near_blocks = neighbour.reshape(NB, blocks, COL_DEV).transpose(1, 0, 2)
    interp_blocks = interp_weight.reshape(NB, blocks, COL_DEV).transpose(1, 0, 2)

    def update(operands):
        ens_block, trans_block, near_block, interp_block = operands
        ens_mean = lax.optimization_barrier(jnp.mean(ens_block, axis=0))
        anomalies = (ens_block - ens_mean[None]).astype(jnp.bfloat16)
        norm_weight = interp_block / lax.optimization_barrier(jnp.sum(interp_block, axis=0))[None, :]
        matches = near_block[:, None, :] == jnp.arange(N_MEMBER, dtype=jnp.int32)[None, :, None]
        pointwise = lax.optimization_barrier(jnp.sum(jnp.where(matches, norm_weight[:, None, :], jnp.zeros_like(norm_weight[:, None, :])), axis=0))

        def accumulate(which, running):
            product = jnp.einsum('kl,kvc->lvc', trans_block[which].astype(jnp.float32), anomalies.astype(jnp.float32), precision=highest)
            return running + product * pointwise[which][None, None, :]
        zero_sum = jnp.zeros((K, NV, COL_DEV), dtype=ens_block.dtype)
        return ens_mean[None] + lax.fori_loop(0, N_MEMBER, accumulate, zero_sum)
    analysed = lax.map(update, (ens_blocks, trans_blocks, near_blocks, interp_blocks))
    return analysed.transpose(1, 2, 0, 3).reshape(K, NV, NCOL)
```

```python
import functools

import jax
import jax.numpy as jnp
from jax import lax
from jax.experimental import pallas as pl
from jax.experimental.pallas import tpu as pltpu
from jax.sharding import PartitionSpec as P

NS_ITERS = 5
CHUNKS = 8
MESH = pl.DeviceIdType.MESH
f32 = jnp.float32
bf16 = jnp.bfloat16


def split(x):
    high = x.astype(bf16)
    return high, (x - high.astype(f32)).astype(bf16)


def mm(x, y):
    return jnp.dot(x, y, preferred_element_type=f32)


def mm_t(x, y):
    return lax.dot_general(x, y, (((1,), (1,)), ((), ())), preferred_element_type=f32)


def mm3(x, y):
    return mm(x[0], y[0]) + (mm(x[0], y[1]) + mm(x[1], y[0]))


def kernel(
    n,
    block,
    ens_ref,
    weight_ref,
    value_ref,
    rinv_ref,
    column_ref,
    rows_ref,
    count_ref,
    near_ref,
    interp_ref,
    out_ref,
    held,
    result_held,
    sums,
    mean,
    anom,
    seen,
    acc,
    hot,
    turn,
    turns,
    sum_send,
    sum_recv,
    turn_send,
    turn_recv,
    own_send,
    own_recv,
    far_send,
    far_recv,
    pass_send,
    pass_recv,
    held_sem,
    result_sem,
):
    me = lax.axis_index("member")
    chips = n // 2
    chip, core = me // 2, lax.rem(me, 2)
    partner = chip * 2 + (1 - core)
    nv = mean.shape[0]
    members = n * block
    group = nv // CHUNKS
    n_obs = weight_ref.shape[1]
    n_set = rows_ref.shape[1]

    def peer(step):
        return lax.rem(me + step, n)

    def far(step):
        return lax.rem(chip + step, chips) * 2 + core

    def came(step):
        return lax.rem(chip + chips - step, chips) * 2 + core

    def span(index):
        return pl.ds(pl.multiple_of(index * block, block), block)

    def remote(src, dst, send, recv, to):
        return pltpu.make_async_remote_copy(
            src_ref=src,
            dst_ref=dst,
            send_sem=send,
            recv_sem=recv,
            device_id={"member": to},
            device_id_type=MESH,
        )

    lanes = held.shape[0]
    loads = [
        pltpu.make_async_copy(
            ens_ref.at[:, :, pl.ds(lane * 128, 128)], held.at[lane], held_sem.at[lane]
        )
        for lane in range(lanes)
    ]
    for copy in loads:
        copy.start()

    barrier = pltpu.get_barrier_semaphore()
    for step in range(1, n):
        pl.semaphore_signal(barrier, inc=1, device_id={"member": peer(step)}, device_id_type=MESH)
    pl.semaphore_wait(barrier, n - 1)

    def view(part, index):
        if part == 0:
            return seen.at[span(index), :]
        return anom.at[pl.ds((part - 1) * group, group), span(index), :]

    def own_copy(part):
        ref = view(part, me)
        return remote(ref, ref, own_send.at[part], own_recv.at[part], partner)

    def far_copy(part, step):
        ref = view(part, me)
        return remote(ref, ref, far_send.at[part, step - 1], far_recv.at[part, step - 1], far(step))

    def pass_copy(part, step):
        ref = view(part, came(step))
        return remote(ref, ref, pass_send.at[part, step - 1], pass_recv.at[part, step - 1], partner)

    def send(part):
        for step in range(1, chips):
            far_copy(part, step).start()
        own_copy(part).start()

    def forward(part):
        for step in range(1, chips):
            far_copy(part, step).wait_recv()
            pass_copy(part, step).start()

    def arrive(part):
        own_copy(part).wait_recv()
        for step in range(1, chips):
            pass_copy(part, step).wait_recv()

    for lane in range(lanes):
        loads[lane].wait()
        total = held[lane, 0]
        for k in range(1, block):
            total = total + held[lane, k]
        sums[me, :, pl.ds(lane * 128, 128)] = total
    sum_copies = [
        remote(sums.at[me], sums.at[me], sum_send.at[step - 1], sum_recv.at[step - 1], peer(step))
        for step in range(1, n)
    ]
    for copy in sum_copies:
        copy.start()
    cols = hot.shape[0]
    hot[...] = jnp.where(
        lax.broadcasted_iota(jnp.int32, (cols, n_obs), 0) == column_ref[...], 1.0, 0.0
    ).astype(bf16)
    for copy in sum_copies:
        copy.wait_recv()
    whole = sums[0]
    for m in range(1, n):
        whole = whole + sums[m]
    mean[...] = whole * (1.0 / members)

    for v in range(nv):
        for lane in range(lanes):
            flat = held.at[lane].reshape(block * nv, 128)
            picked = flat[pl.ds(v, block, stride=nv), :]
            across = pl.ds(lane * 128, 128)
            anom[v, span(me), across] = (picked - mean[pl.ds(v, 1), across]).astype(bf16)
    send(1)

    lift = 8
    for g in range(nv // lift):
        rows = anom[pl.ds(g * lift, lift), span(me), :].reshape(lift * block, cols)
        picked = mm(rows, hot[...])
        part = picked[:block] * weight_ref[pl.ds(g * lift, 1), :]
        for i in range(1, lift):
            part = part + picked[i * block : (i + 1) * block] * weight_ref[pl.ds(g * lift + i, 1), :]
        acc[...] = part if g == 0 else acc[...] + part
    seen[span(me), :] = acc[...].astype(bf16)
    send(0)
    send(2)

    mean_high, mean_low = split(mean[...])
    picked = mm(mean_high, hot[...]) + mm(mean_low, hot[...])
    seen_mean = jnp.sum(picked * weight_ref[...], axis=0, keepdims=True)
    own_row = lax.broadcasted_iota(jnp.int32, (n, 1), 0) == me
    my_rows = jnp.sum(jnp.where(own_row, rows_ref[...], 0), axis=0, keepdims=True)
    my_count = jnp.sum(jnp.where(own_row, count_ref[...], 0), axis=0, keepdims=True)
    live = lax.broadcasted_iota(jnp.int32, (1, n_set), 1) < my_count
    where = jnp.where(live, my_rows, -1)
    match = jnp.where(lax.broadcasted_iota(jnp.int32, (n_obs, n_set), 0) == where, 1.0, 0.0).astype(bf16)
    times = mm_t(jnp.ones((16, n_set), bf16), match)[:1]
    root = jnp.sqrt(times * rinv_ref[...])

    forward(0)
    send(3)
    send(4)
    arrive(0)
    forward(1)

    observed = seen[...].astype(f32)
    rest = jnp.mean(observed, axis=0, keepdims=True)
    scaled = split((observed - rest) * root)
    push = split((value_ref[...] - (seen_mean + rest)) * root)
    eye = jnp.where(
        lax.broadcasted_iota(jnp.int32, (members, members), 0)
        == lax.broadcasted_iota(jnp.int32, (members, members), 1),
        1.0,
        0.0,
    )
    cross = mm_t(scaled[0], scaled[1])
    posterior = (members - 1.0) * eye + (mm_t(scaled[0], scaled[0]) + (cross + mm_t(scaled[1], scaled[0])))
    wide = [jnp.broadcast_to(p, (16, n_obs)) for p in push]
    drive = mm_t(wide[0], scaled[0]) + (mm_t(wide[0], scaled[1]) + mm_t(wide[1], scaled[0]))
    square = jnp.sum(jnp.sum(posterior * posterior, axis=0, keepdims=True), axis=1, keepdims=True)
    norm = jnp.sqrt(square)
    iterate = posterior * (1.0 / norm)
    inverse = None
    for turn_index in range(NS_ITERS):
        step_whole = 1.5 * eye - 0.5 * iterate
        step_now = split(step_whole)
        if inverse is None:
            inverse = step_whole
        else:
            inverse = mm3(split(inverse), step_now)
        if turn_index < NS_ITERS - 1:
            iterate = mm3(split(mm3(split(iterate), step_now)), step_now)
        if turn_index == 2:
            forward(2)
    last = split(inverse)
    weight_row = mm3(split(mm3(split(drive), last)), last)[:1] * (1.0 / norm)
    turn[...] = (inverse * jnp.sqrt((members - 1.0) / norm) + weight_row).astype(bf16)
    turn_copies = [
        remote(
            turn.at[span(peer(step)), :],
            turns.at[span(me), :],
            turn_send.at[step - 1],
            turn_recv.at[step - 1],
            peer(step),
        )
        for step in range(1, n)
    ]
    for copy in turn_copies:
        copy.start()
    for part in range(5, CHUNKS + 1):
        send(part)
    turns[span(me), :] = turn[span(me), :]

    near = near_ref[...]
    share = interp_ref[...] / jnp.sum(interp_ref[...], axis=0, keepdims=True)
    point = [jnp.sum(jnp.where(near == m, share, 0.0), axis=0, keepdims=True) for m in range(n)]
    forward(3)
    for copy in turn_copies:
        copy.wait_recv()

    stores = []
    for part in range(1, CHUNKS + 1):
        if 3 < part + 1 <= CHUNKS:
            forward(part + 1)
        arrive(part)

        for v in range((part - 1) * group, part * group):
            product = mm(turns[...], anom[v])
            result = mean[pl.ds(v, 1), :] + product[:block] * point[0]
            for m in range(1, n):
                result = result + product[m * block : (m + 1) * block] * point[m]
            for lane in range(lanes):
                flat = result_held.at[lane].reshape(block * nv, 128)
                flat[pl.ds(v, block, stride=nv), :] = result[:, lane * 128 : (lane + 1) * 128]
        if part * group % 8 == 0:
            start_row = part * group // 8 * 8 - 8
            for lane in range(lanes):
                store = pltpu.make_async_copy(
                    result_held.at[lane, :, pl.ds(start_row, 8), :],
                    out_ref.at[:, pl.ds(start_row, 8), pl.ds(lane * 128, 128)],
                    result_sem.at[start_row // 8, lane],
                )
                store.start()
                stores.append(store)

    for copy in stores:
        copy.wait()
    for copy in sum_copies + turn_copies:
        copy.wait_send()
    for part in range(CHUNKS + 1):
        own_copy(part).wait_send()
        for step in range(1, chips):
            far_copy(part, step).wait_send()
            pass_copy(part, step).wait_send()


def local(
    ensemble,
    obs_weight,
    obs_value,
    obs_rinv,
    obs_column,
    set_rows,
    set_count,
    neighbour,
    interp_weight,
):
    n = lax.axis_size("member")
    block, nv, cols = ensemble.shape
    n_obs = obs_weight.shape[1]
    members = n * block
    far = max(n // 2 - 1, 1)
    parts = CHUNKS + 1
    dma = pltpu.SemaphoreType.DMA
    flops = 2 * members * members * nv * cols * n // 4 + 2 * block * nv * cols * n_obs
    return pl.pallas_call(
        functools.partial(kernel, n, block),
        out_shape=jax.ShapeDtypeStruct(ensemble.shape, f32),
        in_specs=[pl.BlockSpec(memory_space=pl.ANY)] + [pl.BlockSpec(memory_space=pltpu.VMEM)] * 8,
        out_specs=pl.BlockSpec(memory_space=pl.ANY),
        scratch_shapes=[
            pltpu.VMEM((cols // 128, block, nv, 128), f32),
            pltpu.VMEM((cols // 128, block, nv, 128), f32),
            pltpu.VMEM((n, nv, cols), f32),
            pltpu.VMEM((nv, cols), f32),
            pltpu.VMEM((nv, members, cols), bf16),
            pltpu.VMEM((members, n_obs), bf16),
            pltpu.VMEM((block, n_obs), f32),
            pltpu.VMEM((cols, n_obs), bf16),
            pltpu.VMEM((members, members), bf16),
            pltpu.VMEM((members, members), bf16),
            dma((n - 1,)),
            dma((n - 1,)),
            dma((n - 1,)),
            dma((n - 1,)),
            dma((parts,)),
            dma((parts,)),
            dma((parts, far)),
            dma((parts, far)),
            dma((parts, far)),
            dma((parts, far)),
            dma((cols // 128,)),
            dma((nv // 8, cols // 128)),
        ],
        compiler_params=pltpu.CompilerParams(
            collective_id=0, has_side_effects=True, vmem_limit_bytes=48 * 1024 * 1024
        ),
        cost_estimate=pl.CostEstimate(
            flops=flops, bytes_accessed=8 * block * nv * cols, transcendentals=0
        ),
    )(
        ensemble,
        obs_weight,
        obs_value.reshape(1, n_obs),
        obs_rinv.reshape(1, n_obs),
        obs_column.reshape(1, n_obs),
        set_rows,
        set_count.reshape(-1, 1),
        neighbour,
        interp_weight,
    )


def solution(mesh):
    placed = (
        P("member", None, "space"),
        P(None, "space"),
        P("space"),
        P("space"),
        P("space"),
        P("space", None),
        P("space"),
        P(None, "space"),
        P(None, "space"),
    )
    return jax.shard_map(
        local, mesh=mesh, in_specs=placed, out_specs=P("member", None, "space"), check_vma=False
    )
```

```python
import functools

import jax
import jax.numpy as jnp
from jax import lax
from jax.experimental import pallas as pl
from jax.experimental.pallas import tpu as pltpu
from jax.sharding import PartitionSpec as P

NS_ITERS = 5
CHUNKS = 8
EARLY = 1
MESH = pl.DeviceIdType.MESH
f32 = jnp.float32
bf16 = jnp.bfloat16


def split(x):
    high = x.astype(bf16)
    return high, (x - high.astype(f32)).astype(bf16)


def mm(x, y):
    return jnp.dot(x, y, preferred_element_type=f32)


def mm_t(x, y):
    return lax.dot_general(x, y, (((1,), (1,)), ((), ())), preferred_element_type=f32)


def mm3(x, y):
    return mm(x[0], y[0]) + (mm(x[0], y[1]) + mm(x[1], y[0]))


def kernel(
    n,
    block,
    ens_ref,
    weight_in,
    value_in,
    rinv_in,
    column_in,
    rows_in,
    count_in,
    near_in,
    interp_in,
    out_ref,
    held,
    result_held,
    sums,
    mean,
    anom,
    seen,
    acc,
    hot,
    turn,
    turns,
    sum_send,
    sum_recv,
    turn_send,
    turn_recv,
    own_send,
    own_recv,
    far_send,
    far_recv,
    pass_send,
    pass_recv,
    held_sem,
    result_sem,
    loose,
    shift,
    lean,
    weight_ref,
    value_ref,
    rinv_ref,
    column_ref,
    rows_ref,
    count_ref,
    near_ref,
    interp_ref,
    in_sem,
):
    me = lax.axis_index("member")
    chips = n // 2
    chip, core = me // 2, lax.rem(me, 2)
    partner = chip * 2 + (1 - core)
    nv = mean.shape[0]
    members = n * block
    group = nv // CHUNKS
    n_obs = weight_in.shape[1]
    n_set = rows_in.shape[1]

    def peer(step):
        return lax.rem(me + step, n)

    def far(step):
        return lax.rem(chip + step, chips) * 2 + core

    def came(step):
        return lax.rem(chip + chips - step, chips) * 2 + core

    def span(index):
        return pl.ds(pl.multiple_of(index * block, block), block)

    def remote(src, dst, send, recv, to):
        return pltpu.make_async_remote_copy(
            src_ref=src,
            dst_ref=dst,
            send_sem=send,
            recv_sem=recv,
            device_id={"member": to},
            device_id_type=MESH,
        )

    lanes = held.shape[0]
    loads = [
        pltpu.make_async_copy(
            ens_ref.at[:, :, pl.ds(lane * 128, 128)], held.at[lane], held_sem.at[lane]
        )
        for lane in range(lanes)
    ]
    small = [
        pltpu.make_async_copy(src, dst, in_sem.at[i])
        for i, (src, dst) in enumerate(
            (
                (column_in, column_ref),
                (weight_in, weight_ref),
                (value_in, value_ref),
                (rinv_in, rinv_ref),
                (rows_in, rows_ref),
                (count_in, count_ref),
                (near_in, near_ref),
                (interp_in, interp_ref),
            )
        )
    ]
    for copy in loads + small:
        copy.start()

    barrier = pltpu.get_barrier_semaphore()
    for step in range(1, n):
        pl.semaphore_signal(barrier, inc=1, device_id={"member": peer(step)}, device_id_type=MESH)

    def view(part, index):
        if part == 0:
            return seen.at[span(index), :]
        return anom.at[pl.ds((part - 1) * group, group), span(index), :]

    def own_copy(part):
        ref = view(part, me)
        return remote(ref, ref, own_send.at[part], own_recv.at[part], partner)

    def far_copy(part, step):
        ref = view(part, me)
        return remote(ref, ref, far_send.at[part, step - 1], far_recv.at[part, step - 1], far(step))

    def pass_copy(part, step):
        ref = view(part, came(step))
        return remote(ref, ref, pass_send.at[part, step - 1], pass_recv.at[part, step - 1], partner)

    def send(part):
        for step in range(1, chips):
            far_copy(part, step).start()
        own_copy(part).start()

    def forward(part):
        for step in range(1, chips):
            far_copy(part, step).wait_recv()
            pass_copy(part, step).start()

    def arrive(part):
        own_copy(part).wait_recv()
        for step in range(1, chips):
            pass_copy(part, step).wait_recv()

    def centre(v, about, into, rows):
        for lane in range(lanes):
            flat = held.at[lane].reshape(block * nv, 128)
            picked = flat[pl.ds(v, block, stride=nv), :]
            across = pl.ds(lane * 128, 128)
            into[v, rows, across] = (picked - about[v : v + 1, lane * 128 : (lane + 1) * 128]).astype(bf16)

    for lane in range(lanes):
        loads[lane].wait()
        total = held[lane, 0]
        for k in range(1, block):
            total = total + held[lane, k]
        sums[me, :, pl.ds(lane * 128, 128)] = total
    own_mean = sums[me] * (1.0 / block)
    for v in range(EARLY * group):
        centre(v, own_mean, anom, span(me))
    pl.semaphore_wait(barrier, n - 1)
    sum_copies = [
        remote(sums.at[me], sums.at[me], sum_send.at[step - 1], sum_recv.at[step - 1], peer(step))
        for step in range(1, n)
    ]
    for copy in sum_copies:
        copy.start()
    for part in range(1, EARLY + 1):
        send(part)
    for v in range(nv):
        centre(v, own_mean, loose, pl.ds(0, block))
    for copy in small:
        copy.wait()
    cols = hot.shape[0]
    hot[...] = jnp.where(
        lax.broadcasted_iota(jnp.int32, (cols, n_obs), 0) == column_ref[...], 1.0, 0.0
    ).astype(bf16)

    lift = 8
    for g in range(nv // lift):
        rows = loose[pl.ds(g * lift, lift), :, :].reshape(lift * block, cols)
        picked = mm(rows, hot[...])
        part = picked[:block] * weight_ref[pl.ds(g * lift, 1), :]
        for i in range(1, lift):
            part = part + picked[i * block : (i + 1) * block] * weight_ref[pl.ds(g * lift + i, 1), :]
        acc[...] = part if g == 0 else acc[...] + part
    seen[span(me), :] = acc[...].astype(bf16)
    send(0)

    for copy in sum_copies:
        copy.wait_recv()
    whole = sums[0]
    for m in range(1, n):
        whole = whole + sums[m]
    mean[...] = whole * (1.0 / members)
    middle = mean[...]
    for m in range(n):
        shift[m] = sums[m] * (1.0 / block) - middle
    for v in range(EARLY * group, nv):
        centre(v, middle, anom, span(me))
        if (v + 1) % group == 0 and (v + 1) // group <= EARLY + 2:
            send((v + 1) // group)

    seen_parts = []
    for m in range(n + 1):
        high, low = split(middle if m == n else shift[m])
        picked = mm(high, hot[...]) + mm(low, hot[...])
        seen_parts.append(jnp.sum(picked * weight_ref[...], axis=0, keepdims=True))
    own_row = lax.broadcasted_iota(jnp.int32, (n, 1), 0) == me
    my_rows = jnp.sum(jnp.where(own_row, rows_ref[...], 0), axis=0, keepdims=True)
    own_lane = lax.broadcasted_iota(jnp.int32, (1, n), 1) == me
    my_count = jnp.sum(jnp.where(own_lane, count_ref[...], 0), axis=1, keepdims=True)
    live = lax.broadcasted_iota(jnp.int32, (1, n_set), 1) < my_count
    where = jnp.where(live, my_rows, -1)
    match = jnp.where(lax.broadcasted_iota(jnp.int32, (n_obs, n_set), 0) == where, 1.0, 0.0).astype(bf16)
    times = mm_t(jnp.ones((16, n_set), bf16), match)[:1]
    root = jnp.sqrt(times * rinv_ref[...])

    forward(0)
    forward(1)
    send(EARLY + 3)
    arrive(0)

    observed = jnp.concatenate(
        [seen[pl.ds(m * block, block), :].astype(f32) + seen_parts[m] for m in range(n)], axis=0
    )
    rest = jnp.mean(observed, axis=0, keepdims=True)
    scaled = split((observed - rest) * root)
    push = split((value_ref[...] - (seen_parts[n] + rest)) * root)
    eye = jnp.where(
        lax.broadcasted_iota(jnp.int32, (members, members), 0)
        == lax.broadcasted_iota(jnp.int32, (members, members), 1),
        1.0,
        0.0,
    )
    cross = mm_t(scaled[0], scaled[1])
    posterior = (members - 1.0) * eye + (mm_t(scaled[0], scaled[0]) + (cross + mm_t(scaled[1], scaled[0])))
    wide = [jnp.broadcast_to(p, (16, n_obs)) for p in push]
    drive = mm_t(wide[0], scaled[0]) + (mm_t(wide[0], scaled[1]) + mm_t(wide[1], scaled[0]))
    square = jnp.sum(jnp.sum(posterior * posterior, axis=0, keepdims=True), axis=1, keepdims=True)
    norm = jnp.sqrt(square)
    iterate = posterior * (1.0 / norm)
    inverse = None
    for turn_index in range(NS_ITERS):
        step_whole = 1.5 * eye - 0.5 * iterate
        step_now = split(step_whole)
        if inverse is None:
            inverse = step_whole
        else:
            inverse = mm3(split(inverse), step_now)
        if turn_index < NS_ITERS - 1:
            iterate = mm3(split(mm3(split(iterate), step_now)), step_now)
        if turn_index == 1:
            send(EARLY + 4)
            forward(2)
        if turn_index == 3:
            send(EARLY + 5)
            forward(3)
    last = split(inverse)
    weight_row = mm3(split(mm3(split(drive), last)), last)[:1] * (1.0 / norm)
    turn[...] = (inverse * jnp.sqrt((members - 1.0) / norm) + weight_row).astype(bf16)
    turn_copies = [
        remote(
            turn.at[span(peer(step)), :],
            turns.at[span(me), :],
            turn_send.at[step - 1],
            turn_recv.at[step - 1],
            peer(step),
        )
        for step in range(1, n)
    ]
    for copy in turn_copies:
        copy.start()
    for part in range(EARLY + 6, CHUNKS + 1):
        send(part)
    turns[span(me), :] = turn[span(me), :]

    near = near_ref[...]
    share = interp_ref[...] / jnp.sum(interp_ref[...], axis=0, keepdims=True)
    point = [jnp.sum(jnp.where(near == m, share, 0.0), axis=0, keepdims=True) for m in range(n)]
    forward(4)
    for copy in turn_copies:
        copy.wait_recv()
    for m in range(n):
        block_sums = [
            jnp.sum(
                turns[pl.ds(j * block, block), pl.ds(0, members)].astype(f32)
                * jnp.where(lax.broadcasted_iota(jnp.int32, (1, members), 1) // block == m, 1.0, 0.0),
                axis=1,
                keepdims=True,
            )
            for j in range(n)
        ]
        gathered = block_sums[0] * point[0]
        for j in range(1, n):
            gathered = gathered + block_sums[j] * point[j]
        lean[m] = gathered

    stores = []
    for part in range(1, CHUNKS + 1):
        if 4 < part + 1 <= CHUNKS:
            forward(part + 1)
        arrive(part)

        for v in range((part - 1) * group, part * group):
            product = mm(turns[...], anom[v])
            result = mean[pl.ds(v, 1), :] + product[:block] * point[0]
            for m in range(1, n):
                result = result + product[m * block : (m + 1) * block] * point[m]
            if part <= EARLY:
                for m in range(n):
                    result = result + lean[m] * shift[m, pl.ds(v, 1), :]
            for lane in range(lanes):
                flat = result_held.at[lane].reshape(block * nv, 128)
                flat[pl.ds(v, block, stride=nv), :] = result[:, lane * 128 : (lane + 1) * 128]
        if part * group % 8 == 0:
            start_row = part * group // 8 * 8 - 8
            for lane in range(lanes):
                store = pltpu.make_async_copy(
                    result_held.at[lane, :, pl.ds(start_row, 8), :],
                    out_ref.at[:, pl.ds(start_row, 8), pl.ds(lane * 128, 128)],
                    result_sem.at[start_row // 8, lane],
                )
                store.start()
                stores.append(store)

    for copy in stores:
        copy.wait()
    for copy in sum_copies + turn_copies:
        copy.wait_send()
    for part in range(CHUNKS + 1):
        own_copy(part).wait_send()
        for step in range(1, chips):
            far_copy(part, step).wait_send()
            pass_copy(part, step).wait_send()


def local(
    ensemble,
    obs_weight,
    obs_value,
    obs_rinv,
    obs_column,
    set_rows,
    set_count,
    neighbour,
    interp_weight,
):
    n = lax.axis_size("member")
    block, nv, cols = ensemble.shape
    n_obs = obs_weight.shape[1]
    members = n * block
    far = max(n // 2 - 1, 1)
    parts = CHUNKS + 1
    dma = pltpu.SemaphoreType.DMA
    flops = 2 * members * members * nv * cols * n // 4 + 2 * block * nv * cols * n_obs
    return pl.pallas_call(
        functools.partial(kernel, n, block),
        out_shape=jax.ShapeDtypeStruct(ensemble.shape, f32),
        in_specs=[pl.BlockSpec(memory_space=pltpu.HBM)] * 9,
        out_specs=pl.BlockSpec(memory_space=pl.ANY),
        scratch_shapes=[
            pltpu.VMEM((cols // 128, block, nv, 128), f32),
            pltpu.VMEM((cols // 128, block, nv, 128), f32),
            pltpu.VMEM((n, nv, cols), f32),
            pltpu.VMEM((nv, cols), f32),
            pltpu.VMEM((nv, members, cols), bf16),
            pltpu.VMEM((members, n_obs), bf16),
            pltpu.VMEM((block, n_obs), f32),
            pltpu.VMEM((cols, n_obs), bf16),
            pltpu.VMEM((members, members), bf16),
            pltpu.VMEM((members, members), bf16),
            dma((n - 1,)),
            dma((n - 1,)),
            dma((n - 1,)),
            dma((n - 1,)),
            dma((parts,)),
            dma((parts,)),
            dma((parts, far)),
            dma((parts, far)),
            dma((parts, far)),
            dma((parts, far)),
            dma((cols // 128,)),
            dma((nv // 8, cols // 128)),
            pltpu.VMEM((nv, block, cols), bf16),
            pltpu.VMEM((n, nv, cols), f32),
            pltpu.VMEM((n, block, cols), f32),
            pltpu.VMEM((nv, n_obs), f32),
            pltpu.VMEM((1, n_obs), f32),
            pltpu.VMEM((1, n_obs), f32),
            pltpu.VMEM((1, n_obs), jnp.int32),
            pltpu.VMEM(set_rows.shape, jnp.int32),
            pltpu.VMEM((1, n), jnp.int32),
            pltpu.VMEM(neighbour.shape, jnp.int32),
            pltpu.VMEM(interp_weight.shape, f32),
            dma((8,)),
        ],
        compiler_params=pltpu.CompilerParams(
            collective_id=0, has_side_effects=True, vmem_limit_bytes=60 * 1024 * 1024
        ),
        cost_estimate=pl.CostEstimate(
            flops=flops, bytes_accessed=8 * block * nv * cols, transcendentals=0
        ),
    )(
        ensemble,
        obs_weight,
        obs_value.reshape(1, n_obs),
        obs_rinv.reshape(1, n_obs),
        obs_column.reshape(1, n_obs),
        set_rows,
        set_count.reshape(1, n),
        neighbour,
        interp_weight,
    )


def solution(mesh):
    placed = (
        P("member", None, "space"),
        P(None, "space"),
        P("space"),
        P("space"),
        P("space"),
        P("space", None),
        P("space"),
        P(None, "space"),
        P(None, "space"),
    )
    return jax.shard_map(
        local, mesh=mesh, in_specs=placed, out_specs=P("member", None, "space"), check_vma=False
    )
```

```python
import functools

import jax
import jax.numpy as jnp
from jax import lax
from jax.experimental import pallas as pl
from jax.experimental.pallas import tpu as pltpu
from jax.sharding import PartitionSpec as P

NS_ITERS = 5
CHUNKS = 8
EARLY = 1
MESH = pl.DeviceIdType.MESH
f32 = jnp.float32
bf16 = jnp.bfloat16


def split(x):
    high = x.astype(bf16)
    return high, (x - high.astype(f32)).astype(bf16)


def mm(x, y):
    return jnp.dot(x, y, preferred_element_type=f32)


def mm_t(x, y):
    return lax.dot_general(x, y, (((1,), (1,)), ((), ())), preferred_element_type=f32)


def mm3(x, y):
    return mm(x[0], y[0]) + (mm(x[0], y[1]) + mm(x[1], y[0]))


def kernel(
    n,
    block,
    ens_ref,
    weight_in,
    value_in,
    rinv_in,
    column_in,
    rows_in,
    count_in,
    near_in,
    interp_in,
    out_ref,
    held,
    result_held,
    sums,
    mean,
    anom,
    seen,
    acc,
    hot,
    turn,
    turns,
    sum_send,
    sum_recv,
    turn_send,
    turn_recv,
    own_send,
    own_recv,
    far_send,
    far_recv,
    pass_send,
    pass_recv,
    held_sem,
    result_sem,
    loose,
    shift,
    lean,
    weight_ref,
    value_ref,
    rinv_ref,
    column_ref,
    rows_ref,
    count_ref,
    near_ref,
    interp_ref,
    in_sem,
):
    me = lax.axis_index("member")
    chips = n // 2
    chip, core = me // 2, lax.rem(me, 2)
    partner = chip * 2 + (1 - core)
    nv = mean.shape[0]
    members = n * block
    group = nv // CHUNKS
    n_obs = weight_in.shape[1]
    n_set = rows_in.shape[1]

    def peer(step):
        return lax.rem(me + step, n)

    def far(step):
        return lax.rem(chip + step, chips) * 2 + core

    def came(step):
        return lax.rem(chip + chips - step, chips) * 2 + core

    def span(index):
        return pl.ds(pl.multiple_of(index * block, block), block)

    def remote(src, dst, send, recv, to):
        return pltpu.make_async_remote_copy(
            src_ref=src,
            dst_ref=dst,
            send_sem=send,
            recv_sem=recv,
            device_id={"member": to},
            device_id_type=MESH,
        )

    lanes = held.shape[0]
    loads = [
        pltpu.make_async_copy(
            ens_ref.at[:, :, pl.ds(lane * 128, 128)], held.at[lane], held_sem.at[lane]
        )
        for lane in range(lanes)
    ]
    small = [
        pltpu.make_async_copy(src, dst, in_sem.at[i])
        for i, (src, dst) in enumerate(
            (
                (column_in, column_ref),
                (weight_in, weight_ref),
                (value_in, value_ref),
                (rinv_in, rinv_ref),
                (rows_in, rows_ref),
                (count_in, count_ref),
                (near_in, near_ref),
                (interp_in, interp_ref),
            )
        )
    ]
    for copy in loads + small:
        copy.start()

    barrier = pltpu.get_barrier_semaphore()
    for step in range(1, n):
        pl.semaphore_signal(barrier, inc=1, device_id={"member": peer(step)}, device_id_type=MESH)

    def view(part, index):
        if part == 0:
            return seen.at[span(index), :]
        return anom.at[pl.ds((part - 1) * group, group), span(index), :]

    def own_copy(part):
        ref = view(part, me)
        return remote(ref, ref, own_send.at[part], own_recv.at[part], partner)

    def far_copy(part, step):
        ref = view(part, me)
        return remote(ref, ref, far_send.at[part, step - 1], far_recv.at[part, step - 1], far(step))

    def pass_copy(part, step):
        ref = view(part, came(step))
        return remote(ref, ref, pass_send.at[part, step - 1], pass_recv.at[part, step - 1], partner)

    def send(part):
        for step in range(1, chips):
            far_copy(part, step).start()
        own_copy(part).start()

    def forward(part):
        for step in range(1, chips):
            far_copy(part, step).wait_recv()
            pass_copy(part, step).start()

    def arrive(part):
        own_copy(part).wait_recv()
        for step in range(1, chips):
            pass_copy(part, step).wait_recv()

    def centre(v, about, into, rows):
        for lane in range(lanes):
            flat = held.at[lane].reshape(block * nv, 128)
            picked = flat[pl.ds(v, block, stride=nv), :]
            across = pl.ds(lane * 128, 128)
            into[v, rows, across] = (picked - about[v : v + 1, lane * 128 : (lane + 1) * 128]).astype(bf16)

    for lane in range(lanes):
        loads[lane].wait()
        total = held[lane, 0]
        for k in range(1, block):
            total = total + held[lane, k]
        sums[me, :, pl.ds(lane * 128, 128)] = total
    own_mean = sums[me] * (1.0 / block)
    for v in range(EARLY * group):
        centre(v, own_mean, anom, span(me))
    pl.semaphore_wait(barrier, n - 1)
    sum_copies = [
        remote(sums.at[me], sums.at[me], sum_send.at[step - 1], sum_recv.at[step - 1], peer(step))
        for step in range(1, n)
    ]
    for copy in sum_copies:
        copy.start()
    for part in range(1, EARLY + 1):
        send(part)
    for v in range(nv):
        centre(v, own_mean, loose, pl.ds(0, block))
    for copy in small:
        copy.wait()
    cols = hot.shape[0]
    hot[...] = jnp.where(
        lax.broadcasted_iota(jnp.int32, (cols, n_obs), 0) == column_ref[...], 1.0, 0.0
    ).astype(bf16)

    lift = 8
    for g in range(nv // lift):
        rows = loose[pl.ds(g * lift, lift), :, :].reshape(lift * block, cols)
        picked = mm(rows, hot[...])
        part = picked[:block] * weight_ref[pl.ds(g * lift, 1), :]
        for i in range(1, lift):
            part = part + picked[i * block : (i + 1) * block] * weight_ref[pl.ds(g * lift + i, 1), :]
        acc[...] = part if g == 0 else acc[...] + part
    seen[span(me), :] = acc[...].astype(bf16)
    send(0)

    for copy in sum_copies:
        copy.wait_recv()
    whole = sums[0]
    for m in range(1, n):
        whole = whole + sums[m]
    mean[...] = whole * (1.0 / members)
    middle = mean[...]
    for m in range(n):
        shift[m] = sums[m] * (1.0 / block) - middle
    for v in range(EARLY * group, nv):
        centre(v, middle, anom, span(me))
        if (v + 1) % group == 0 and (v + 1) // group <= EARLY + 2:
            send((v + 1) // group)
    forward(0)
    send(EARLY + 3)

    high, low = split(jnp.concatenate([shift[m] for m in range(n)] + [middle], axis=0))
    picked = mm(jnp.concatenate([high, low], axis=0), hot[...])
    seen_parts = []
    for m in range(n + 1):
        both = picked[m * nv : (m + 1) * nv] + picked[(n + 1 + m) * nv : (n + 2 + m) * nv]
        seen_parts.append(jnp.sum(both * weight_ref[...], axis=0, keepdims=True))
    own_row = lax.broadcasted_iota(jnp.int32, (n, 1), 0) == me
    my_rows = jnp.sum(jnp.where(own_row, rows_ref[...], 0), axis=0, keepdims=True)
    own_lane = lax.broadcasted_iota(jnp.int32, (1, n), 1) == me
    my_count = jnp.sum(jnp.where(own_lane, count_ref[...], 0), axis=1, keepdims=True)
    live = lax.broadcasted_iota(jnp.int32, (1, n_set), 1) < my_count
    where = jnp.where(live, my_rows, -1)
    match = jnp.where(lax.broadcasted_iota(jnp.int32, (n_obs, n_set), 0) == where, 1.0, 0.0).astype(bf16)
    times = mm_t(jnp.ones((16, n_set), bf16), match)[:1]
    root = jnp.sqrt(times * rinv_ref[...])

    arrive(0)
    forward(1)
    send(EARLY + 4)

    observed = jnp.concatenate(
        [seen[pl.ds(m * block, block), :].astype(f32) + seen_parts[m] for m in range(n)], axis=0
    )
    rest = jnp.mean(observed, axis=0, keepdims=True)
    scaled = split((observed - rest) * root)
    push = split((value_ref[...] - (seen_parts[n] + rest)) * root)
    eye = jnp.where(
        lax.broadcasted_iota(jnp.int32, (members, members), 0)
        == lax.broadcasted_iota(jnp.int32, (members, members), 1),
        1.0,
        0.0,
    )
    left = [
        jnp.concatenate([scaled[i], jnp.broadcast_to(push[i], (16, n_obs))], axis=0) for i in range(2)
    ]
    grown = mm_t(left[0], scaled[0]) + (mm_t(left[0], scaled[1]) + mm_t(left[1], scaled[0]))
    posterior = (members - 1.0) * eye + grown[:members]
    drive = grown[members:]
    square = jnp.sum(jnp.sum(posterior * posterior, axis=0, keepdims=True), axis=1, keepdims=True)
    norm = jnp.sqrt(square)
    iterate = posterior * (1.0 / norm)
    inverse = None
    for turn_index in range(NS_ITERS):
        step_whole = 1.5 * eye - 0.5 * iterate
        step_now = split(step_whole)
        final = turn_index == NS_ITERS - 1
        if inverse is None:
            inverse = step_whole
            if not final:
                iterate = mm3(split(iterate), step_now)
        elif final:
            inverse = mm3(split(inverse), step_now)
        else:
            both = mm3(split(jnp.concatenate([iterate, inverse], axis=0)), step_now)
            iterate = both[:members]
            inverse = both[members:]
        if not final:
            iterate = mm3(split(iterate), step_now)
        if turn_index == 0:
            send(EARLY + 5)
        if turn_index == 1:
            forward(2)
        if turn_index == 2:
            send(EARLY + 6)
        if turn_index == 3:
            forward(3)
    last = split(inverse)
    weight_row = mm3(split(mm3(split(drive), last)), last)[:1] * (1.0 / norm)
    turn[...] = (inverse * jnp.sqrt((members - 1.0) / norm) + weight_row).astype(bf16)
    turn_copies = [
        remote(
            turn.at[span(peer(step)), :],
            turns.at[span(me), :],
            turn_send.at[step - 1],
            turn_recv.at[step - 1],
            peer(step),
        )
        for step in range(1, n)
    ]
    for copy in turn_copies:
        copy.start()
    for part in range(EARLY + 7, CHUNKS + 1):
        send(part)
    turns[span(me), :] = turn[span(me), :]

    near = near_ref[...]
    share = interp_ref[...] / jnp.sum(interp_ref[...], axis=0, keepdims=True)
    point = [jnp.sum(jnp.where(near == m, share, 0.0), axis=0, keepdims=True) for m in range(n)]
    forward(4)
    for copy in turn_copies:
        copy.wait_recv()
    for m in range(n):
        block_sums = [
            jnp.sum(
                turns[pl.ds(j * block, block), pl.ds(0, members)].astype(f32)
                * jnp.where(lax.broadcasted_iota(jnp.int32, (1, members), 1) // block == m, 1.0, 0.0),
                axis=1,
                keepdims=True,
            )
            for j in range(n)
        ]
        gathered = block_sums[0] * point[0]
        for j in range(1, n):
            gathered = gathered + block_sums[j] * point[j]
        lean[m] = gathered

    stores = []
    for part in range(1, CHUNKS + 1):
        if 4 < part + 1 <= CHUNKS:
            forward(part + 1)
        arrive(part)

        for v in range((part - 1) * group, part * group):
            product = mm(turns[...], anom[v])
            result = mean[pl.ds(v, 1), :] + product[:block] * point[0]
            for m in range(1, n):
                result = result + product[m * block : (m + 1) * block] * point[m]
            if part <= EARLY:
                for m in range(n):
                    result = result + lean[m] * shift[m, pl.ds(v, 1), :]
            for lane in range(lanes):
                flat = result_held.at[lane].reshape(block * nv, 128)
                flat[pl.ds(v, block, stride=nv), :] = result[:, lane * 128 : (lane + 1) * 128]
        if part * group % 8 == 0:
            start_row = part * group // 8 * 8 - 8
            for lane in range(lanes):
                store = pltpu.make_async_copy(
                    result_held.at[lane, :, pl.ds(start_row, 8), :],
                    out_ref.at[:, pl.ds(start_row, 8), pl.ds(lane * 128, 128)],
                    result_sem.at[start_row // 8, lane],
                )
                store.start()
                stores.append(store)

    for copy in stores:
        copy.wait()
    for copy in sum_copies + turn_copies:
        copy.wait_send()
    for part in range(CHUNKS + 1):
        own_copy(part).wait_send()
        for step in range(1, chips):
            far_copy(part, step).wait_send()
            pass_copy(part, step).wait_send()


def local(
    ensemble,
    obs_weight,
    obs_value,
    obs_rinv,
    obs_column,
    set_rows,
    set_count,
    neighbour,
    interp_weight,
):
    n = lax.axis_size("member")
    block, nv, cols = ensemble.shape
    n_obs = obs_weight.shape[1]
    members = n * block
    far = max(n // 2 - 1, 1)
    parts = CHUNKS + 1
    dma = pltpu.SemaphoreType.DMA
    flops = 2 * members * members * nv * cols * n // 4 + 2 * block * nv * cols * n_obs
    return pl.pallas_call(
        functools.partial(kernel, n, block),
        out_shape=jax.ShapeDtypeStruct(ensemble.shape, f32),
        in_specs=[pl.BlockSpec(memory_space=pltpu.HBM)] * 9,
        out_specs=pl.BlockSpec(memory_space=pl.ANY),
        scratch_shapes=[
            pltpu.VMEM((cols // 128, block, nv, 128), f32),
            pltpu.VMEM((cols // 128, block, nv, 128), f32),
            pltpu.VMEM((n, nv, cols), f32),
            pltpu.VMEM((nv, cols), f32),
            pltpu.VMEM((nv, members, cols), bf16),
            pltpu.VMEM((members, n_obs), bf16),
            pltpu.VMEM((block, n_obs), f32),
            pltpu.VMEM((cols, n_obs), bf16),
            pltpu.VMEM((members, members), bf16),
            pltpu.VMEM((members, members), bf16),
            dma((n - 1,)),
            dma((n - 1,)),
            dma((n - 1,)),
            dma((n - 1,)),
            dma((parts,)),
            dma((parts,)),
            dma((parts, far)),
            dma((parts, far)),
            dma((parts, far)),
            dma((parts, far)),
            dma((cols // 128,)),
            dma((nv // 8, cols // 128)),
            pltpu.VMEM((nv, block, cols), bf16),
            pltpu.VMEM((n, nv, cols), f32),
            pltpu.VMEM((n, block, cols), f32),
            pltpu.VMEM((nv, n_obs), f32),
            pltpu.VMEM((1, n_obs), f32),
            pltpu.VMEM((1, n_obs), f32),
            pltpu.VMEM((1, n_obs), jnp.int32),
            pltpu.VMEM(set_rows.shape, jnp.int32),
            pltpu.VMEM((1, n), jnp.int32),
            pltpu.VMEM(neighbour.shape, jnp.int32),
            pltpu.VMEM(interp_weight.shape, f32),
            dma((8,)),
        ],
        compiler_params=pltpu.CompilerParams(
            collective_id=0, has_side_effects=True, vmem_limit_bytes=48 * 1024 * 1024
        ),
        cost_estimate=pl.CostEstimate(
            flops=flops, bytes_accessed=8 * block * nv * cols, transcendentals=0
        ),
    )(
        *[
            pltpu.with_memory_space_constraint(operand, pltpu.HBM)
            for operand in (
                ensemble,
                obs_weight,
                obs_value.reshape(1, n_obs),
                obs_rinv.reshape(1, n_obs),
                obs_column.reshape(1, n_obs),
                set_rows,
                set_count.reshape(1, n),
                neighbour,
                interp_weight,
            )
        ]
    )


def solution(mesh):
    placed = (
        P("member", None, "space"),
        P(None, "space"),
        P("space"),
        P("space"),
        P("space"),
        P("space", None),
        P("space"),
        P(None, "space"),
        P(None, "space"),
    )
    return jax.shard_map(
        local, mesh=mesh, in_specs=placed, out_specs=P("member", None, "space"), check_vma=False
    )
```

```python
import functools

import jax
import jax.numpy as jnp
from jax import lax
from jax.experimental import pallas as pl
from jax.experimental.pallas import tpu as pltpu
from jax.sharding import PartitionSpec as P

NS_ITERS = 5
CHUNKS = 8
EARLY = 1
MESH = pl.DeviceIdType.MESH
f32 = jnp.float32
bf16 = jnp.bfloat16


def split(x):
    high = x.astype(bf16)
    return high, (x - high.astype(f32)).astype(bf16)


def mm(x, y):
    return jnp.dot(x, y, preferred_element_type=f32)


def mm_t(x, y):
    return lax.dot_general(x, y, (((1,), (1,)), ((), ())), preferred_element_type=f32)


def mm3(x, y):
    return mm(x[0], y[0]) + (mm(x[0], y[1]) + mm(x[1], y[0]))


def kernel(
    n,
    block,
    ens_ref,
    weight_in,
    value_in,
    rinv_in,
    column_in,
    rows_in,
    count_in,
    near_in,
    interp_in,
    out_ref,
    held,
    result_held,
    sums,
    mean,
    anom,
    seen,
    acc,
    hot,
    turn,
    turns,
    turn_send,
    turn_recv,
    own_send,
    own_recv,
    far_send,
    far_recv,
    pass_send,
    pass_recv,
    held_sem,
    result_sem,
    loose,
    shift,
    lean,
    weight_ref,
    value_ref,
    rinv_ref,
    column_ref,
    rows_ref,
    count_ref,
    near_ref,
    interp_ref,
    in_sem,
):
    me = lax.axis_index("member")
    chips = n // 2
    chip, core = me // 2, lax.rem(me, 2)
    partner = chip * 2 + (1 - core)
    nv = mean.shape[0]
    members = n * block
    group = nv // CHUNKS
    n_obs = weight_in.shape[1]
    n_set = rows_in.shape[1]

    def peer(step):
        return lax.rem(me + step, n)

    def far(step):
        return lax.rem(chip + step, chips) * 2 + core

    def came(step):
        return lax.rem(chip + chips - step, chips) * 2 + core

    def span(index):
        return pl.ds(pl.multiple_of(index * block, block), block)

    def remote(src, dst, send, recv, to):
        return pltpu.make_async_remote_copy(
            src_ref=src,
            dst_ref=dst,
            send_sem=send,
            recv_sem=recv,
            device_id={"member": to},
            device_id_type=MESH,
        )

    lanes = held.shape[0]
    loads = [
        pltpu.make_async_copy(
            ens_ref.at[:, :, pl.ds(lane * 128, 128)], held.at[lane], held_sem.at[lane]
        )
        for lane in range(lanes)
    ]
    small = [
        pltpu.make_async_copy(src, dst, in_sem.at[i])
        for i, (src, dst) in enumerate(
            (
                (column_in, column_ref),
                (weight_in, weight_ref),
                (value_in, value_ref),
                (rinv_in, rinv_ref),
                (rows_in, rows_ref),
                (count_in, count_ref),
                (near_in, near_ref),
                (interp_in, interp_ref),
            )
        )
    ]
    for copy in loads + small:
        copy.start()

    barrier = pltpu.get_barrier_semaphore()
    for step in range(1, n):
        pl.semaphore_signal(barrier, inc=1, device_id={"member": peer(step)}, device_id_type=MESH)

    def view(part, index):
        if part == 0:
            return seen.at[span(index), :]
        if part == CHUNKS + 1:
            return sums.at[index]
        return anom.at[pl.ds((part - 1) * group, group), span(index), :]

    def own_copy(part):
        ref = view(part, me)
        return remote(ref, ref, own_send.at[part], own_recv.at[part], partner)

    def far_copy(part, step):
        ref = view(part, me)
        return remote(ref, ref, far_send.at[part, step - 1], far_recv.at[part, step - 1], far(step))

    def pass_copy(part, step):
        ref = view(part, came(step))
        return remote(ref, ref, pass_send.at[part, step - 1], pass_recv.at[part, step - 1], partner)

    def send(part):
        for step in range(1, chips):
            far_copy(part, step).start()
        own_copy(part).start()

    def forward(part):
        for step in range(1, chips):
            far_copy(part, step).wait_recv()
            pass_copy(part, step).start()

    def arrive(part):
        own_copy(part).wait_recv()
        for step in range(1, chips):
            pass_copy(part, step).wait_recv()

    def centre(v, about, into, rows):
        for lane in range(lanes):
            flat = held.at[lane].reshape(block * nv, 128)
            picked = flat[pl.ds(v, block, stride=nv), :]
            across = pl.ds(lane * 128, 128)
            into[v, rows, across] = (picked - about[v : v + 1, lane * 128 : (lane + 1) * 128]).astype(bf16)

    for lane in range(lanes):
        loads[lane].wait()
        total = held[lane, 0]
        for k in range(1, block):
            total = total + held[lane, k]
        sums[me, :, pl.ds(lane * 128, 128)] = total
    own_mean = sums[me] * (1.0 / block)
    for v in range(EARLY * group):
        centre(v, own_mean, anom, span(me))
    pl.semaphore_wait(barrier, n - 1)
    send(CHUNKS + 1)
    for part in range(1, EARLY + 1):
        send(part)
    for v in range(nv):
        centre(v, own_mean, loose, pl.ds(0, block))
    for copy in small:
        copy.wait()
    cols = hot.shape[0]
    hot[...] = jnp.where(
        lax.broadcasted_iota(jnp.int32, (cols, n_obs), 0) == column_ref[...], 1.0, 0.0
    ).astype(bf16)

    forward(CHUNKS + 1)
    lift = 8
    for g in range(nv // lift):
        rows = loose[pl.ds(g * lift, lift), :, :].reshape(lift * block, cols)
        picked = mm(rows, hot[...])
        part = picked[:block] * weight_ref[pl.ds(g * lift, 1), :]
        for i in range(1, lift):
            part = part + picked[i * block : (i + 1) * block] * weight_ref[pl.ds(g * lift + i, 1), :]
        acc[...] = part if g == 0 else acc[...] + part
    seen[span(me), :] = acc[...].astype(bf16)
    send(0)

    arrive(CHUNKS + 1)
    whole = sums[0]
    for m in range(1, n):
        whole = whole + sums[m]
    mean[...] = whole * (1.0 / members)
    middle = mean[...]
    for m in range(n):
        shift[m] = sums[m] * (1.0 / block) - middle
    for v in range(EARLY * group, nv):
        centre(v, middle, anom, span(me))
        if (v + 1) % group == 0 and (v + 1) // group <= EARLY + 2:
            send((v + 1) // group)
    forward(0)

    high, low = split(jnp.concatenate([shift[m] for m in range(n)] + [middle], axis=0))
    picked = mm(jnp.concatenate([high, low], axis=0), hot[...])
    seen_parts = []
    for m in range(n + 1):
        both = picked[m * nv : (m + 1) * nv] + picked[(n + 1 + m) * nv : (n + 2 + m) * nv]
        seen_parts.append(jnp.sum(both * weight_ref[...], axis=0, keepdims=True))
    own_row = lax.broadcasted_iota(jnp.int32, (n, 1), 0) == me
    my_rows = jnp.sum(jnp.where(own_row, rows_ref[...], 0), axis=0, keepdims=True)
    own_lane = lax.broadcasted_iota(jnp.int32, (1, n), 1) == me
    my_count = jnp.sum(jnp.where(own_lane, count_ref[...], 0), axis=1, keepdims=True)
    live = lax.broadcasted_iota(jnp.int32, (1, n_set), 1) < my_count
    where = jnp.where(live, my_rows, -1)
    match = jnp.where(lax.broadcasted_iota(jnp.int32, (n_obs, n_set), 0) == where, 1.0, 0.0).astype(bf16)
    times = mm_t(jnp.ones((16, n_set), bf16), match)[:1]
    root = jnp.sqrt(times * rinv_ref[...])

    arrive(0)
    forward(1)
    send(EARLY + 3)

    observed = jnp.concatenate(
        [seen[pl.ds(m * block, block), :].astype(f32) + seen_parts[m] for m in range(n)], axis=0
    )
    rest = jnp.mean(observed, axis=0, keepdims=True)
    scaled = split((observed - rest) * root)
    push = split((value_ref[...] - (seen_parts[n] + rest)) * root)
    eye = jnp.where(
        lax.broadcasted_iota(jnp.int32, (members, members), 0)
        == lax.broadcasted_iota(jnp.int32, (members, members), 1),
        1.0,
        0.0,
    )
    left = [
        jnp.concatenate([scaled[i], jnp.broadcast_to(push[i], (16, n_obs))], axis=0) for i in range(2)
    ]
    grown = mm_t(left[0], scaled[0]) + (mm_t(left[0], scaled[1]) + mm_t(left[1], scaled[0]))
    posterior = (members - 1.0) * eye + grown[:members]
    drive = grown[members:]
    square = jnp.sum(jnp.sum(posterior * posterior, axis=0, keepdims=True), axis=1, keepdims=True)
    norm = jnp.sqrt(square)
    iterate = posterior * (1.0 / norm)
    inverse = None
    for turn_index in range(NS_ITERS):
        step_whole = 1.5 * eye - 0.5 * iterate
        step_now = split(step_whole)
        final = turn_index == NS_ITERS - 1
        if inverse is None:
            inverse = step_whole
            if not final:
                iterate = mm3(split(iterate), step_now)
        elif final:
            inverse = mm3(split(inverse), step_now)
        else:
            both = mm3(split(jnp.concatenate([iterate, inverse], axis=0)), step_now)
            iterate = both[:members]
            inverse = both[members:]
        if not final:
            iterate = mm3(split(iterate), step_now)
        if turn_index == 1:
            send(EARLY + 4)
            forward(2)
        if turn_index == 3:
            send(EARLY + 5)
        if turn_index == 3:
            forward(3)
    last = split(inverse)
    weight_row = mm3(split(mm3(split(drive), last)), last)[:1] * (1.0 / norm)
    turn[...] = (inverse * jnp.sqrt((members - 1.0) / norm) + weight_row).astype(bf16)
    turn_copies = [
        remote(
            turn.at[span(peer(step)), :],
            turns.at[span(me), :],
            turn_send.at[step - 1],
            turn_recv.at[step - 1],
            peer(step),
        )
        for step in range(1, n)
    ]
    for copy in turn_copies:
        copy.start()
    for part in range(EARLY + 6, CHUNKS + 1):
        send(part)
    turns[span(me), :] = turn[span(me), :]

    near = near_ref[...]
    share = interp_ref[...] / jnp.sum(interp_ref[...], axis=0, keepdims=True)
    point = [jnp.sum(jnp.where(near == m, share, 0.0), axis=0, keepdims=True) for m in range(n)]
    forward(4)
    for copy in turn_copies:
        copy.wait_recv()
    for m in range(n):
        block_sums = [
            jnp.sum(
                turns[pl.ds(j * block, block), pl.ds(0, members)].astype(f32)
                * jnp.where(lax.broadcasted_iota(jnp.int32, (1, members), 1) // block == m, 1.0, 0.0),
                axis=1,
                keepdims=True,
            )
            for j in range(n)
        ]
        gathered = block_sums[0] * point[0]
        for j in range(1, n):
            gathered = gathered + block_sums[j] * point[j]
        lean[m] = gathered

    stores = []
    for part in range(1, CHUNKS + 1):
        if 4 < part + 1 <= CHUNKS:
            forward(part + 1)
        arrive(part)

        first = (part - 1) * group
        wide = mm(turns[...], jnp.concatenate([anom[first + i] for i in range(group)], axis=1))
        for i in range(group):
            v = first + i
            product = wide[:, i * cols : (i + 1) * cols]
            result = mean[pl.ds(v, 1), :] + product[:block] * point[0]
            for m in range(1, n):
                result = result + product[m * block : (m + 1) * block] * point[m]
            if part <= EARLY:
                for m in range(n):
                    result = result + lean[m] * shift[m, pl.ds(v, 1), :]
            for lane in range(lanes):
                flat = result_held.at[lane].reshape(block * nv, 128)
                flat[pl.ds(v, block, stride=nv), :] = result[:, lane * 128 : (lane + 1) * 128]
        if part * group % 8 == 0:
            start_row = part * group // 8 * 8 - 8
            for lane in range(lanes):
                store = pltpu.make_async_copy(
                    result_held.at[lane, :, pl.ds(start_row, 8), :],
                    out_ref.at[:, pl.ds(start_row, 8), pl.ds(lane * 128, 128)],
                    result_sem.at[start_row // 8, lane],
                )
                store.start()
                stores.append(store)

    for copy in stores:
        copy.wait()
    for copy in turn_copies:
        copy.wait_send()
    for part in range(CHUNKS + 2):
        own_copy(part).wait_send()
        for step in range(1, chips):
            far_copy(part, step).wait_send()
            pass_copy(part, step).wait_send()


def local(
    ensemble,
    obs_weight,
    obs_value,
    obs_rinv,
    obs_column,
    set_rows,
    set_count,
    neighbour,
    interp_weight,
):
    n = lax.axis_size("member")
    block, nv, cols = ensemble.shape
    n_obs = obs_weight.shape[1]
    members = n * block
    far = max(n // 2 - 1, 1)
    parts = CHUNKS + 2
    dma = pltpu.SemaphoreType.DMA
    flops = 2 * members * members * nv * cols * n // 4 + 2 * block * nv * cols * n_obs
    return pl.pallas_call(
        functools.partial(kernel, n, block),
        out_shape=jax.ShapeDtypeStruct(ensemble.shape, f32),
        in_specs=[pl.BlockSpec(memory_space=pltpu.HBM)] * 9,
        out_specs=pl.BlockSpec(memory_space=pl.ANY),
        scratch_shapes=[
            pltpu.VMEM((cols // 128, block, nv, 128), f32),
            pltpu.VMEM((cols // 128, block, nv, 128), f32),
            pltpu.VMEM((n, nv, cols), f32),
            pltpu.VMEM((nv, cols), f32),
            pltpu.VMEM((nv, members, cols), bf16),
            pltpu.VMEM((members, n_obs), bf16),
            pltpu.VMEM((block, n_obs), f32),
            pltpu.VMEM((cols, n_obs), bf16),
            pltpu.VMEM((members, members), bf16),
            pltpu.VMEM((members, members), bf16),
            dma((n - 1,)),
            dma((n - 1,)),
            dma((parts,)),
            dma((parts,)),
            dma((parts, far)),
            dma((parts, far)),
            dma((parts, far)),
            dma((parts, far)),
            dma((cols // 128,)),
            dma((nv // 8, cols // 128)),
            pltpu.VMEM((nv, block, cols), bf16),
            pltpu.VMEM((n, nv, cols), f32),
            pltpu.VMEM((n, block, cols), f32),
            pltpu.VMEM((nv, n_obs), f32),
            pltpu.VMEM((1, n_obs), f32),
            pltpu.VMEM((1, n_obs), f32),
            pltpu.VMEM((1, n_obs), jnp.int32),
            pltpu.VMEM(set_rows.shape, jnp.int32),
            pltpu.VMEM((1, n), jnp.int32),
            pltpu.VMEM(neighbour.shape, jnp.int32),
            pltpu.VMEM(interp_weight.shape, f32),
            dma((8,)),
        ],
        compiler_params=pltpu.CompilerParams(
            collective_id=0, has_side_effects=True, vmem_limit_bytes=48 * 1024 * 1024
        ),
        cost_estimate=pl.CostEstimate(
            flops=flops, bytes_accessed=8 * block * nv * cols, transcendentals=0
        ),
    )(
        *[
            pltpu.with_memory_space_constraint(operand, pltpu.HBM)
            for operand in (
                ensemble,
                obs_weight,
                obs_value.reshape(1, n_obs),
                obs_rinv.reshape(1, n_obs),
                obs_column.reshape(1, n_obs),
                set_rows,
                set_count.reshape(1, n),
                neighbour,
                interp_weight,
            )
        ]
    )


def solution(mesh):
    placed = (
        P("member", None, "space"),
        P(None, "space"),
        P("space"),
        P("space"),
        P("space"),
        P("space", None),
        P("space"),
        P(None, "space"),
        P(None, "space"),
    )
    return jax.shard_map(
        local, mesh=mesh, in_specs=placed, out_specs=P("member", None, "space"), check_vma=False
    )
```

```python
import functools

import jax
import jax.numpy as jnp
from jax import lax
from jax.experimental import pallas as pl
from jax.experimental.pallas import tpu as pltpu
from jax.sharding import PartitionSpec as P

NS_ITERS = 5
CHUNKS = 8
EARLY = 1
MESH = pl.DeviceIdType.MESH
f32 = jnp.float32
bf16 = jnp.bfloat16


def split(x):
    high = x.astype(bf16)
    return high, (x - high.astype(f32)).astype(bf16)


def mm(x, y):
    return jnp.dot(x, y, preferred_element_type=f32)


def mm_t(x, y):
    return lax.dot_general(x, y, (((1,), (1,)), ((), ())), preferred_element_type=f32)


def mm3(x, y):
    return mm(x[0], y[0]) + (mm(x[0], y[1]) + mm(x[1], y[0]))


def kernel(
    n,
    block,
    ens_ref,
    weight_in,
    value_in,
    rinv_in,
    column_in,
    rows_in,
    count_in,
    near_in,
    interp_in,
    out_ref,
    held,
    result_held,
    sums,
    mean,
    anom,
    seen,
    acc,
    hot,
    turn,
    turns,
    turn_send,
    turn_recv,
    own_send,
    own_recv,
    far_send,
    far_recv,
    pass_send,
    pass_recv,
    held_sem,
    result_sem,
    loose,
    shift,
    lean,
    weight_ref,
    value_ref,
    rinv_ref,
    column_ref,
    rows_ref,
    count_ref,
    near_ref,
    interp_ref,
    in_sem,
):
    me = lax.axis_index("member")
    chips = n // 2
    chip, core = me // 2, lax.rem(me, 2)
    partner = chip * 2 + (1 - core)
    nv = mean.shape[0]
    members = n * block
    group = nv // CHUNKS
    n_obs = weight_in.shape[1]
    n_set = rows_in.shape[1]

    def peer(step):
        return lax.rem(me + step, n)

    def far(step):
        return lax.rem(chip + step, chips) * 2 + core

    def came(step):
        return lax.rem(chip + chips - step, chips) * 2 + core

    def span(index):
        return pl.ds(pl.multiple_of(index * block, block), block)

    def remote(src, dst, send, recv, to):
        return pltpu.make_async_remote_copy(
            src_ref=src,
            dst_ref=dst,
            send_sem=send,
            recv_sem=recv,
            device_id={"member": to},
            device_id_type=MESH,
        )

    lanes = held.shape[0]
    loads = [
        pltpu.make_async_copy(
            ens_ref.at[:, :, pl.ds(lane * 128, 128)], held.at[lane], held_sem.at[lane]
        )
        for lane in range(lanes)
    ]
    small = [
        pltpu.make_async_copy(src, dst, in_sem.at[i])
        for i, (src, dst) in enumerate(
            (
                (column_in, column_ref),
                (weight_in, weight_ref),
                (value_in, value_ref),
                (rinv_in, rinv_ref),
                (rows_in, rows_ref),
                (count_in, count_ref),
                (near_in, near_ref),
                (interp_in, interp_ref),
            )
        )
    ]
    for copy in loads + small:
        copy.start()

    barrier = pltpu.get_barrier_semaphore()
    for step in range(1, n):
        pl.semaphore_signal(barrier, inc=1, device_id={"member": peer(step)}, device_id_type=MESH)

    def view(part, index):
        if part == 0:
            return seen.at[span(index), :]
        if part == CHUNKS + 1:
            return sums.at[index]
        return anom.at[pl.ds((part - 1) * group, group), span(index), :]

    def own_copy(part):
        ref = view(part, me)
        return remote(ref, ref, own_send.at[part], own_recv.at[part], partner)

    def far_copy(part, step):
        ref = view(part, me)
        return remote(ref, ref, far_send.at[part, step - 1], far_recv.at[part, step - 1], far(step))

    def pass_copy(part, step):
        ref = view(part, came(step))
        return remote(ref, ref, pass_send.at[part, step - 1], pass_recv.at[part, step - 1], partner)

    def send(part):
        for step in range(1, chips):
            far_copy(part, step).start()
        own_copy(part).start()

    def forward(part):
        for step in range(1, chips):
            far_copy(part, step).wait_recv()
            pass_copy(part, step).start()

    def arrive(part):
        own_copy(part).wait_recv()
        for step in range(1, chips):
            pass_copy(part, step).wait_recv()

    def centre(v, about, into, rows):
        for lane in range(lanes):
            flat = held.at[lane].reshape(block * nv, 128)
            picked = flat[pl.ds(v, block, stride=nv), :]
            across = pl.ds(lane * 128, 128)
            into[v, rows, across] = (picked - about[v : v + 1, lane * 128 : (lane + 1) * 128]).astype(bf16)

    for lane in range(lanes):
        loads[lane].wait()
        total = held[lane, 0]
        for k in range(1, block):
            total = total + held[lane, k]
        sums[me, :, pl.ds(lane * 128, 128)] = total
    own_mean = sums[me] * (1.0 / block)
    for v in range(EARLY * group):
        centre(v, own_mean, anom, span(me))
    pl.semaphore_wait(barrier, n - 1)
    send(CHUNKS + 1)
    for part in range(1, EARLY + 1):
        send(part)
    for v in range(nv):
        centre(v, own_mean, loose, pl.ds(0, block))
    for copy in small:
        copy.wait()
    cols = hot.shape[0]
    hot[...] = jnp.where(
        lax.broadcasted_iota(jnp.int32, (cols, n_obs), 0) == column_ref[...], 1.0, 0.0
    ).astype(bf16)

    forward(CHUNKS + 1)
    lift = 8
    for g in range(nv // lift):
        rows = loose[pl.ds(g * lift, lift), :, :].reshape(lift * block, cols)
        picked = mm(rows, hot[...])
        part = picked[:block] * weight_ref[pl.ds(g * lift, 1), :]
        for i in range(1, lift):
            part = part + picked[i * block : (i + 1) * block] * weight_ref[pl.ds(g * lift + i, 1), :]
        acc[...] = part if g == 0 else acc[...] + part
    seen[span(me), :] = acc[...].astype(bf16)
    send(0)

    arrive(CHUNKS + 1)
    whole = sums[0]
    for m in range(1, n):
        whole = whole + sums[m]
    mean[...] = whole * (1.0 / members)
    middle = mean[...]
    for m in range(n):
        shift[m] = sums[m] * (1.0 / block) - middle
    def centre_part(part):
        for v in range((part - 1) * group, part * group):
            centre(v, middle, anom, span(me))

    for part in range(EARLY + 1, EARLY + 3):
        centre_part(part)
        send(part)
    forward(0)

    high, low = split(jnp.concatenate([shift[m] for m in range(n)] + [middle], axis=0))
    picked = mm(jnp.concatenate([high, low], axis=0), hot[...])
    seen_parts = []
    for m in range(n + 1):
        both = picked[m * nv : (m + 1) * nv] + picked[(n + 1 + m) * nv : (n + 2 + m) * nv]
        seen_parts.append(jnp.sum(both * weight_ref[...], axis=0, keepdims=True))
    own_row = lax.broadcasted_iota(jnp.int32, (n, 1), 0) == me
    my_rows = jnp.sum(jnp.where(own_row, rows_ref[...], 0), axis=0, keepdims=True)
    own_lane = lax.broadcasted_iota(jnp.int32, (1, n), 1) == me
    my_count = jnp.sum(jnp.where(own_lane, count_ref[...], 0), axis=1, keepdims=True)
    live = lax.broadcasted_iota(jnp.int32, (1, n_set), 1) < my_count
    where = jnp.where(live, my_rows, -1)
    match = jnp.where(lax.broadcasted_iota(jnp.int32, (n_obs, n_set), 0) == where, 1.0, 0.0).astype(bf16)
    times = mm_t(jnp.ones((16, n_set), bf16), match)[:1]
    root = jnp.sqrt(times * rinv_ref[...])

    centre_part(EARLY + 3)
    arrive(0)
    forward(1)
    send(EARLY + 3)

    observed = jnp.concatenate(
        [seen[pl.ds(m * block, block), :].astype(f32) + seen_parts[m] for m in range(n)], axis=0
    )
    rest = jnp.mean(observed, axis=0, keepdims=True)
    scaled = split((observed - rest) * root)
    push = split((value_ref[...] - (seen_parts[n] + rest)) * root)
    eye = jnp.where(
        lax.broadcasted_iota(jnp.int32, (members, members), 0)
        == lax.broadcasted_iota(jnp.int32, (members, members), 1),
        1.0,
        0.0,
    )
    left = [
        jnp.concatenate([scaled[i], jnp.broadcast_to(push[i], (16, n_obs))], axis=0) for i in range(2)
    ]
    grown = mm_t(left[0], scaled[0]) + (mm_t(left[0], scaled[1]) + mm_t(left[1], scaled[0]))
    posterior = (members - 1.0) * eye + grown[:members]
    drive = grown[members:]
    square = jnp.sum(jnp.sum(posterior * posterior, axis=0, keepdims=True), axis=1, keepdims=True)
    norm = jnp.sqrt(square)
    iterate = posterior * (1.0 / norm)
    inverse = None
    for turn_index in range(NS_ITERS):
        step_whole = 1.5 * eye - 0.5 * iterate
        step_now = split(step_whole)
        final = turn_index == NS_ITERS - 1
        if EARLY + 4 + turn_index <= CHUNKS:
            centre_part(EARLY + 4 + turn_index)
        if inverse is None:
            inverse = step_whole
            if not final:
                iterate = mm3(split(iterate), step_now)
        elif final:
            inverse = mm3(split(inverse), step_now)
        else:
            both = mm3(split(jnp.concatenate([iterate, inverse], axis=0)), step_now)
            iterate = both[:members]
            inverse = both[members:]
        if not final:
            iterate = mm3(split(iterate), step_now)
        if turn_index == 1:
            send(EARLY + 4)
            forward(2)
        if turn_index == 3:
            send(EARLY + 5)
        if turn_index == 3:
            forward(3)
    last = split(inverse)
    weight_row = mm3(split(mm3(split(drive), last)), last)[:1] * (1.0 / norm)
    turn[...] = (inverse * jnp.sqrt((members - 1.0) / norm) + weight_row).astype(bf16)
    turn_copies = [
        remote(
            turn.at[span(peer(step)), :],
            turns.at[span(me), :],
            turn_send.at[step - 1],
            turn_recv.at[step - 1],
            peer(step),
        )
        for step in range(1, n)
    ]
    for copy in turn_copies:
        copy.start()
    for part in range(EARLY + 6, CHUNKS + 1):
        send(part)
    turns[span(me), :] = turn[span(me), :]

    near = near_ref[...]
    share = interp_ref[...] / jnp.sum(interp_ref[...], axis=0, keepdims=True)
    point = [jnp.sum(jnp.where(near == m, share, 0.0), axis=0, keepdims=True) for m in range(n)]
    forward(4)
    for copy in turn_copies:
        copy.wait_recv()
    for m in range(n):
        block_sums = [
            jnp.sum(
                turns[pl.ds(j * block, block), pl.ds(0, members)].astype(f32)
                * jnp.where(lax.broadcasted_iota(jnp.int32, (1, members), 1) // block == m, 1.0, 0.0),
                axis=1,
                keepdims=True,
            )
            for j in range(n)
        ]
        gathered = block_sums[0] * point[0]
        for j in range(1, n):
            gathered = gathered + block_sums[j] * point[j]
        lean[m] = gathered

    stores = []
    for part in range(1, CHUNKS + 1):
        if 4 < part + 1 <= CHUNKS:
            forward(part + 1)
        arrive(part)

        first = (part - 1) * group
        wide = mm(turns[...], jnp.concatenate([anom[first + i] for i in range(group)], axis=1))
        for i in range(group):
            v = first + i
            product = wide[:, i * cols : (i + 1) * cols]
            result = mean[pl.ds(v, 1), :] + product[:block] * point[0]
            for m in range(1, n):
                result = result + product[m * block : (m + 1) * block] * point[m]
            if part <= EARLY:
                for m in range(n):
                    result = result + lean[m] * shift[m, pl.ds(v, 1), :]
            for lane in range(lanes):
                flat = result_held.at[lane].reshape(block * nv, 128)
                flat[pl.ds(v, block, stride=nv), :] = result[:, lane * 128 : (lane + 1) * 128]
        if part * group % 8 == 0:
            start_row = part * group // 8 * 8 - 8
            for lane in range(lanes):
                store = pltpu.make_async_copy(
                    result_held.at[lane, :, pl.ds(start_row, 8), :],
                    out_ref.at[:, pl.ds(start_row, 8), pl.ds(lane * 128, 128)],
                    result_sem.at[start_row // 8, lane],
                )
                store.start()
                stores.append(store)

    for copy in stores:
        copy.wait()
    for copy in turn_copies:
        copy.wait_send()
    for part in range(CHUNKS + 2):
        own_copy(part).wait_send()
        for step in range(1, chips):
            far_copy(part, step).wait_send()
            pass_copy(part, step).wait_send()


def local(
    ensemble,
    obs_weight,
    obs_value,
    obs_rinv,
    obs_column,
    set_rows,
    set_count,
    neighbour,
    interp_weight,
):
    n = lax.axis_size("member")
    block, nv, cols = ensemble.shape
    n_obs = obs_weight.shape[1]
    members = n * block
    far = max(n // 2 - 1, 1)
    parts = CHUNKS + 2
    dma = pltpu.SemaphoreType.DMA
    flops = 2 * members * members * nv * cols * n // 4 + 2 * block * nv * cols * n_obs
    return pl.pallas_call(
        functools.partial(kernel, n, block),
        out_shape=jax.ShapeDtypeStruct(ensemble.shape, f32),
        in_specs=[pl.BlockSpec(memory_space=pltpu.HBM)] * 9,
        out_specs=pl.BlockSpec(memory_space=pl.ANY),
        scratch_shapes=[
            pltpu.VMEM((cols // 128, block, nv, 128), f32),
            pltpu.VMEM((cols // 128, block, nv, 128), f32),
            pltpu.VMEM((n, nv, cols), f32),
            pltpu.VMEM((nv, cols), f32),
            pltpu.VMEM((nv, members, cols), bf16),
            pltpu.VMEM((members, n_obs), bf16),
            pltpu.VMEM((block, n_obs), f32),
            pltpu.VMEM((cols, n_obs), bf16),
            pltpu.VMEM((members, members), bf16),
            pltpu.VMEM((members, members), bf16),
            dma((n - 1,)),
            dma((n - 1,)),
            dma((parts,)),
            dma((parts,)),
            dma((parts, far)),
            dma((parts, far)),
            dma((parts, far)),
            dma((parts, far)),
            dma((cols // 128,)),
            dma((nv // 8, cols // 128)),
            pltpu.VMEM((nv, block, cols), bf16),
            pltpu.VMEM((n, nv, cols), f32),
            pltpu.VMEM((n, block, cols), f32),
            pltpu.VMEM((nv, n_obs), f32),
            pltpu.VMEM((1, n_obs), f32),
            pltpu.VMEM((1, n_obs), f32),
            pltpu.VMEM((1, n_obs), jnp.int32),
            pltpu.VMEM(set_rows.shape, jnp.int32),
            pltpu.VMEM((1, n), jnp.int32),
            pltpu.VMEM(neighbour.shape, jnp.int32),
            pltpu.VMEM(interp_weight.shape, f32),
            dma((8,)),
        ],
        compiler_params=pltpu.CompilerParams(
            collective_id=0, has_side_effects=True, vmem_limit_bytes=48 * 1024 * 1024
        ),
        cost_estimate=pl.CostEstimate(
            flops=flops, bytes_accessed=8 * block * nv * cols, transcendentals=0
        ),
    )(
        *[
            pltpu.with_memory_space_constraint(operand, pltpu.HBM)
            for operand in (
                ensemble,
                obs_weight,
                obs_value.reshape(1, n_obs),
                obs_rinv.reshape(1, n_obs),
                obs_column.reshape(1, n_obs),
                set_rows,
                set_count.reshape(1, n),
                neighbour,
                interp_weight,
            )
        ]
    )


def solution(mesh):
    placed = (
        P("member", None, "space"),
        P(None, "space"),
        P("space"),
        P("space"),
        P("space"),
        P("space", None),
        P("space"),
        P(None, "space"),
        P(None, "space"),
    )
    return jax.shard_map(
        local, mesh=mesh, in_specs=placed, out_specs=P("member", None, "space"), check_vma=False
    )
```
